512 devices in a mesh: bin: 64 (over z, y), off: 8 (over x, core).
Axes of the slice: x: 4, y: 8, z: 8, core: 2. Of those that a mesh axis runs over, the one named last changes fastest.
Arguments:
- traces: float32 [8, 8192, 1536], P('off', 'bin'), may hold values from -6 to 6
- trace_dest: int32 [8, 8192, 1], P('off', 'bin'), may hold values from 0 to 63; in each aligned block of 128 rows (0 to 127, 128 to 255, ..., all dimensions but the last counted through in order) at most 6 rows name the same one
- trace_bin: int32 [8, 8192], P('off', 'bin'), may hold values from 0 to 31
- trace_class: int32 [8, 8192], P('off', 'bin'), may hold values from 0 to 7
- trace_fold: int32 [8, 8192], P('off', 'bin'), may hold values from 1 to 4
- filters: float32 [8, 48], replicated, may hold values from -0.3 to 0.3
- predictor: float32 [16, 1024], P(None, 'off'), may hold values from -0.4 to 0.4
Outputs:
- error_spectrum: float32 [2048, 1024], P('bin', 'off')
The draws below stay inside these ranges and needn't reach their ends.
Inputs may be any that keep to these rules, and one draw needn't show every extreme that they name: `trace_dest`: in the 128 traces of one device (aligned blocks of rows, groups taken in order) no value is named by more than 6 traces, a bound that some block reaches.
All inputs are finite; a program needn't handle non-finite values.
Results may differ from the reference program's by a relative error of at most 0.0001.
Values sent between devices are 32-bit elements; how exact they have to be, the bound alone decides.
A program may use at most 128 MiB of HBM per device.

```python
import math
import jax
import jax.numpy as jnp
import numpy as np
from jax import lax

SAMPLES = 1536
TAPS = 48
LAGS = 16
FREQS = 512
CLASSES = 8
TR_DEV = 128
BIN_DEV = 32
CAP = 6
GROUPS = 8
TRACES = 8192
N_BIN = 64


def set_ends(array, key, least, largest):
    longest = array.shape.index(max(array.shape))
    spots = []
    for shift in (0, 1):
        where = [jax.random.randint(jax.random.fold_in(key, axis), (), 0, length) for axis, length in enumerate(array.shape)]
        where[longest] = (where[longest] + shift) % array.shape[longest]
        spots.append(tuple(where))
    return array.at[spots[0]].set(least).at[spots[1]].set(largest)


def shard_levels(own_key, dims, pieces, least, high):
    factor_of = 1.0
    for axis_at, blocks in pieces:
        draws = jax.random.uniform(jax.random.fold_in(jax.random.fold_in(own_key, 6), axis_at), (blocks,), jnp.float32, least / len(pieces), high / len(pieces))
        factor_of = factor_of * jnp.repeat(jnp.exp(draws), dims[axis_at] // blocks).reshape((-1,) + (1,) * (len(dims) - 1 - axis_at))
    return factor_of


def routed_block(rng, own, number, rows, number_of, top, bound, slope):
    sequence = jax.random.permutation(rng, number_of)
    heavy_load, common = shares(number_of, rows * top, bound, slope, True), shares(number_of, rows * top, bound, slope, False)
    places = jnp.arange(number_of)

    def named(tallies, turn):
        used = int((tallies > 0).sum())
        fixed = max(1, used // 4)
        shifted = fixed + (places - fixed + turn * (used - fixed)) % max(1, number_of - fixed)
        return jnp.zeros((number_of,), jnp.int32).at[sequence[jnp.where(places < fixed, places, shifted)]].set(jnp.asarray(tallies, jnp.int32))

    tallies = jnp.where(number % 4 == 0, named(heavy_load, number // 4), named(common, number - number // 4 - 1))
    mixed = jax.random.permutation(jax.random.fold_in(own, 3), number_of)
    giver, taker = mixed[0:number_of // 2 * 2:2], mixed[1:number_of // 2 * 2:2]
    margin = jnp.minimum(tallies[giver] - 1, bound - tallies[taker]) // 2
    margin = jnp.where((giver == sequence[0]) | (taker == sequence[0]) | (tallies[taker] == 0), 0, jnp.maximum(margin, 0))
    shifted = jax.random.randint(jax.random.fold_in(own, 4), (number_of // 2,), 0, 1 << 20) % (margin + 1)
    tallies = tallies.at[giver].add(-shifted).at[taker].add(shifted)
    labels = jnp.searchsorted(jnp.cumsum(tallies), jnp.arange(rows * top), side="right").astype(jnp.int32)
    listing = labels.reshape(top, rows).T
    listing = listing[jax.random.permutation(jax.random.fold_in(own, 1), rows)]
    turn = jax.random.randint(jax.random.fold_in(own, 2), (rows, 1), 0, top)
    return jnp.take_along_axis(listing, (jnp.arange(top)[None, :] + turn) % top, axis=1)


def shares(amount, total, most, slope, full):
    loads = [(1 << 20) // math.isqrt(rank ** slope) + 1 for rank in range(1, amount + 1)]
    largest = most if full else min(most, max(-(-total // amount), total * loads[0] // sum(loads)))
    least = 1 if total - largest >= amount - 1 else 0
    counts, surplus = [largest] + [least] * (amount - 1), total - largest - least * (amount - 1)
    while surplus > 0:
        candidates = [i for i in range(1, amount) if counts[i] < largest] or [i for i in range(1, amount) if counts[i] < most]
        pool, remaining = sum([loads[i] for i in candidates]), surplus
        for i in candidates:
            extra = min(most - counts[i], max(1, remaining * loads[i] // pool), surplus)
            counts[i] = counts[i] + extra
            surplus = surplus - extra
    return np.array(counts)


def normal_values(own_key, shape, deviation, bound, shards=(), held_as=jnp.bfloat16):
    loudness = shard_levels(own_key, shape, shards, -0.22, 0.18) if shards else 1.0
    drawn = jax.random.normal(own_key, shape, jnp.float32) * deviation * loudness
    return jnp.minimum(jnp.maximum(drawn, -bound), bound).astype(held_as)


def setup_inputs(seed: int = 0) -> dict:
    streams_of = jax.random.split(jax.random.key(seed), 8)
    traces = normal_values(streams_of[0], (GROUPS, TRACES, SAMPLES), 1.0, 6.0, ((0, 8), (1, 64)), jnp.float32)
    trace_dest_keys = jax.random.split(jax.random.fold_in(streams_of[1], 1), GROUPS * TRACES // TR_DEV)
    trace_dest_turns = jax.random.permutation(jax.random.fold_in(streams_of[1], 3), GROUPS * TRACES // TR_DEV)
    trace_dest = jax.vmap(lambda own, number: routed_block(jax.random.fold_in(streams_of[1], 2), own, number, TR_DEV, N_BIN, 1, CAP, 2))(trace_dest_keys, trace_dest_turns).reshape((GROUPS, TRACES, 1))
    trace_bin = set_ends(jax.random.randint(streams_of[2], (GROUPS, TRACES), 0, BIN_DEV), jax.random.fold_in(streams_of[2], 1), 0, BIN_DEV - 1).astype(jnp.int32)
    trace_class = set_ends(jax.random.randint(streams_of[3], (GROUPS, TRACES), 0, CLASSES), jax.random.fold_in(streams_of[3], 1), 0, CLASSES - 1).astype(jnp.int32)
    trace_fold = set_ends(jax.random.randint(streams_of[4], (GROUPS, TRACES), 1, 5), jax.random.fold_in(streams_of[4], 1), 1, 4).astype(jnp.int32)
    filters = normal_values(streams_of[5], (CLASSES, TAPS), 0.08, 0.3, (), jnp.float32)
    predictor = normal_values(streams_of[6], (LAGS, 2 * FREQS), 0.1, 0.4, ((1, 8),), jnp.float32)
    return dict(traces=traces, trace_dest=trace_dest, trace_bin=trace_bin, trace_class=trace_class, trace_fold=trace_fold, filters=filters, predictor=predictor)


def deconvolve(records, per_trace):
    tap_count = per_trace.shape[1]
    samples = records.shape[1]
    padded = jnp.pad(records, ((0, 0), (tap_count, 0)))
    result = records
    for shift_by in range(1, tap_count + 1):
        result = result - per_trace[:, shift_by - 1:shift_by] * padded[:, tap_count - shift_by:tap_count - shift_by + samples]
    return result

def reference(traces, trace_dest, trace_bin, trace_class, trace_fold, filters, predictor):
    bin_count = BIN_DEV * N_BIN

    def one_group(carry, parts):
        records, targets, bin_slots, class_ids, fold_counts = parts
        cleaned = deconvolve(records, filters[class_ids])
        placed = targets[:, 0] * BIN_DEV + bin_slots
        weights = fold_counts.astype(jnp.float32)
        stacked = carry[0] + jax.ops.segment_sum(weights[:, None] * cleaned, placed, num_segments=bin_count)
        fold_total = carry[1] + jax.ops.segment_sum(weights, placed, num_segments=bin_count)
        return ((stacked, fold_total), None)
    start = (jnp.zeros((bin_count, SAMPLES), jnp.float32), jnp.zeros((bin_count,), jnp.float32))
    (stacked, fold_total), _ = lax.scan(one_group, start, (traces, trace_dest, trace_bin, trace_class, trace_fold))
    normal = stacked / jnp.sqrt(1.0 + fold_total)[:, None]
    spectrum = jnp.fft.rfft(normal, axis=1)[:, :FREQS]
    spec_real = spectrum.real / math.sqrt(SAMPLES)
    spec_imag = spectrum.imag / math.sqrt(SAMPLES)
    coeff_real = predictor[:, 0::2]
    coeff_imag = predictor[:, 1::2]
    pad_real = jnp.pad(spec_real, ((LAGS, 0), (0, 0)))
    pad_imag = jnp.pad(spec_imag, ((LAGS, 0), (0, 0)))
    guess_real = jnp.zeros_like(spec_real)
    guess_imag = jnp.zeros_like(spec_imag)
    for lag_index in range(1, LAGS + 1):
        lagged_real = pad_real[LAGS - lag_index:LAGS - lag_index + bin_count]
        lagged_imag = pad_imag[LAGS - lag_index:LAGS - lag_index + bin_count]
        guess_real = guess_real + coeff_real[lag_index - 1] * lagged_real - coeff_imag[lag_index - 1] * lagged_imag
        guess_imag = guess_imag + coeff_real[lag_index - 1] * lagged_imag + coeff_imag[lag_index - 1] * lagged_real
    error_spectrum = jnp.stack([spec_real - guess_real, spec_imag - guess_imag], axis=-1)
    return error_spectrum.reshape(bin_count, 2 * FREQS)
```

```python
import math

import jax
import jax.numpy as jnp
import ml_dtypes
import numpy as np
from jax import lax
from jax.experimental import pallas as pl
from jax.experimental.pallas import tpu as pltpu
from jax.sharding import PartitionSpec as P

SAMPLES = 1536
HALF = SAMPLES // 2
TAPS = 48
LAGS = 16
BIN_DEV = 32
TR = 128
NZ, NY, NO = 8, 8, 8
GB = NY * BIN_DEV
WIDE = GB + 128
ROWS = 16
MESH = pl.DeviceIdType.MESH
F32, BF16 = jnp.float32, jnp.bfloat16


def split(v):
    high = v.astype(BF16)
    return high, (v - high.astype(F32)).astype(BF16)


def np_split(v):
    high = v.astype(np.float32).astype(ml_dtypes.bfloat16)
    low = (v - high.astype(np.float64)).astype(np.float32).astype(ml_dtypes.bfloat16)
    return high, low


def local_freqs():
    s, m = np.arange(NY)[:, None], np.arange(8)[None, :]
    return 2 * (8 * (s % (NY // 2)) + m) + (s >= NY // 2)


def tables():
    freqs = np.arange(NO)[:, None, None] * (NY * 8) + local_freqs()[None]

    def waves(count):
        phase = freqs[..., None] * np.arange(count) % SAMPLES
        angle = 2.0 * np.pi / SAMPLES * phase
        return np.stack([np.cos(angle), -np.sin(angle)], axis=2)

    main = waves(HALF) / math.sqrt(SAMPLES)
    main = main.reshape(NO, 2, NY // 2 * ROWS, HALF)
    main = np.concatenate(np_split(main), axis=2)
    high, low = np_split(waves(64).reshape(NO, NY * ROWS, 64))
    short = np.concatenate([high, low, high, np.zeros_like(high)], axis=2)
    place = np.zeros((NY * ROWS, NY * ROWS), np.float32)
    cols = 2 * local_freqs()[:, None, :] + np.arange(2)[None, :, None]
    place[np.arange(NY * ROWS), cols.reshape(-1)] = 1
    return main, short, place.astype(ml_dtypes.bfloat16)


def dot(a, b, da, db):
    return lax.dot_general(a, b, (((da,), (db,)), ((), ())), preferred_element_type=F32)


def kernel(
    traces, dest, slot, cls, fold, filt, pred, tab, gtab, place, out,
    xv, tv, gv, x2, pt, rv, rhs, lab0, lab1, lab2, sbuf, rbuf, lhs, hot, acc,
    obuf, obox, fbuf, fbox, ebuf, ebox, cv, cb, res,
    xsem, tsem, gsem, l1s, l1r, l2s, l2r, asend, arecv, bsend, brecv, fsend, frecv, esend, erecv,
):
    b, o = lax.axis_index("bin"), lax.axis_index("off")
    z, y = lax.div(b, NY), lax.rem(b, NY)

    def at(zz, yy, oo):
        return {"bin": zz * NY + yy, "off": oo}

    def remote(src, dst, ss, rs, where):
        return pltpu.make_async_remote_copy(
            src_ref=src, dst_ref=dst, send_sem=ss, recv_sem=rs, device_id=where, device_id_type=MESH
        )

    def await_bytes(ref, sem):
        pltpu.make_async_copy(ref, ref, sem).wait()

    pltpu.make_async_copy(traces.at[0], xv, xsem).start()

    def load(do, c):
        oo = lax.rem(o + do, NO)
        pltpu.make_async_copy(tab.at[oo], tv.at[do], tsem.at[do]).start()
        pltpu.make_async_copy(gtab.at[oo], gv.at[do], gsem.at[do]).start()
        return c

    lax.fori_loop(0, NO, load, 0)

    barrier = pltpu.get_barrier_semaphore()

    def greet(i, c):
        where = at(z, lax.rem(y + lax.rem(i, NY), NY), lax.rem(o + lax.div(i, NY), NO))
        pl.semaphore_signal(barrier, inc=1, device_id=where, device_id_type=MESH)
        return c

    def greet_z(dz, c):
        pl.semaphore_signal(
            barrier, inc=1, device_id=at(lax.rem(z + dz, NZ), y, o), device_id_type=MESH
        )
        return c

    lax.fori_loop(1, NO * NY, greet, 0)
    lax.fori_loop(1, NZ, greet_z, 0)
    lab0[0:1, :] = dest[...] * BIN_DEV + slot[...]
    lab0[1:2, :] = fold[...]
    pl.semaphore_wait(barrier, NO * NY - 1 + NZ - 1)

    pltpu.make_async_copy(lab0, lab1.at[o], l1r).start()

    def tell_off(do, c):
        remote(lab0, lab1.at[o], l1s, l1r, at(z, y, lax.rem(o + do, NO))).start()
        return c

    lax.fori_loop(1, NO, tell_off, 0)

    pltpu.make_async_copy(traces.at[0], xv, xsem).wait()
    first, second = xv[:, :HALF], xv[:, HALF:]
    for parity, v in ((0, first + second), (1, first - second)):
        high, low = split(v)
        x2[parity, 0:TR] = high
        x2[parity, TR : 2 * TR] = low
    pt[0:TAPS] = xv[:, SAMPLES - 128 :].T[128 - TAPS :]
    pt[TAPS:] = jnp.zeros((TAPS, TR), F32)
    class_hot = (lax.broadcasted_iota(jnp.int32, (8, TR), 0) == cls[...]).astype(F32)
    taps = lax.dot_general(
        filt[...].T, class_hot, (((1,), (0,)), ((), ())),
        precision=lax.Precision.HIGHEST, preferred_element_type=F32,
    )
    rv[...] = jnp.zeros_like(rv)
    rv[1 : TAPS + 1, 0:TR] = taps
    wrap = jnp.zeros((TAPS, TR), F32)
    for k in range(1, TAPS + 1):
        wrap = wrap + rv[k : k + 1, 0:TR] * pt[TAPS - k : 2 * TAPS - k]
    rv[0:TAPS, TR:] = wrap * (1.0 / math.sqrt(SAMPLES))
    high, low = split(rv[...])
    rhs[0:64] = high
    rhs[64:128] = high
    rhs[128:192] = low
    rhs[192:256] = jnp.zeros((64, 2 * TR), BF16)

    await_bytes(lab1, l1r)
    pltpu.make_async_copy(lab1, lab2.at[y], l2r).start()

    def tell_y(dy, c):
        remote(lab1, lab2.at[y], l2s, l2r, at(z, lax.rem(y + dy, NY), o)).start()
        return c

    lax.fori_loop(1, NY, tell_y, 0)

    weight = fold[...].astype(F32)
    part = NY // 2 * ROWS

    def transform(do, c):
        oo = lax.rem(o + do, NO)
        pltpu.make_async_copy(tab.at[oo], tv.at[do], tsem.at[do]).wait()
        pltpu.make_async_copy(gtab.at[oo], gv.at[do], gsem.at[do]).wait()
        short = dot(gv[do], rhs[...], 1, 0)
        for parity in range(2):
            four = dot(tv[do, parity], x2[parity], 1, 1)
            spec = (four[:part, :TR] + four[part:, TR:]) + (four[:part, TR:] + four[part:, :TR])
            for i in range(NY // 2):
                s = parity * (NY // 2) + i
                xr, xi = spec[i * ROWS : i * ROWS + 8], spec[i * ROWS + 8 : i * ROWS + 16]
                own = short[s * ROWS : (s + 1) * ROWS]
                gr, gi = 1.0 - own[:8, :TR], -own[8:, :TR]
                sbuf[do * NY + s, 0:8] = (xr * gr - xi * gi + own[:8, TR:]) * weight
                sbuf[do * NY + s, 8:16] = (xr * gi + xi * gr + own[8:, TR:]) * weight

        def send(dy, c):
            yy = lax.rem(y + dy, NY)
            src, dst = sbuf.at[do * NY + yy], rbuf.at[do * NY + dy]
            own = (do == 0) & (dy == 0)

            @pl.when(own)
            def _():
                pltpu.make_async_copy(src, dst, arecv.at[do]).start()

            @pl.when(jnp.logical_not(own))
            def _():
                remote(src, dst, asend, arecv.at[do], at(z, yy, oo)).start()

            return c

        lax.fori_loop(0, NY, send, 0)
        return c

    lax.fori_loop(0, NO, transform, 0)

    rest, coeff = pred[...], jnp.zeros((NY * ROWS, LAGS), F32)
    for _ in range(3):
        high = rest.astype(BF16)
        rest = rest - high.astype(F32)
        coeff = coeff + dot(place[...], high, 1, 1)
    cv[...] = coeff
    own = cv[pl.ds(pl.multiple_of(y * ROWS, ROWS), ROWS), :]
    for lag in range(LAGS):
        cb[lag] = jnp.broadcast_to(own[:, lag : lag + 1], (ROWS, 128))

    await_bytes(lab2, l2r)
    acc[...] = jnp.zeros_like(acc)
    which = lax.broadcasted_iota(jnp.int32, (GB, TR), 0)
    which8 = lax.broadcasted_iota(jnp.int32, (16, TR), 0)

    def stack(g, c):
        await_bytes(rbuf.at[pl.ds(g * NY, NY)], arecv.at[g])
        oo = lax.rem(o - g + NO, NO)
        for dy in range(NY):
            yy = lax.rem(y - dy + NY, NY)
            names = lab2[yy, oo, 0:1, :]
            folds = lab2[yy, oo, 1:2, :].astype(F32)
            upper, lower = lax.shift_right_logical(names, int(math.log2(GB))), names & (GB - 1)
            high, low = split(rbuf[g * NY + dy])
            high, low = high.astype(F32), low.astype(F32)
            lanes = slice(dy * TR, (dy + 1) * TR)
            for zz in range(NZ):
                here = upper == zz
                lhs[zz * ROWS : (zz + 1) * ROWS, lanes] = jnp.where(here, high, 0.0).astype(BF16)
                lhs[(NZ + zz) * ROWS : (NZ + zz + 1) * ROWS, lanes] = jnp.where(
                    here, low, 0.0
                ).astype(BF16)
            lhs[2 * NZ * ROWS :, lanes] = jnp.where(which8 == upper, folds, 0.0).astype(BF16)
            hot[:, lanes] = jnp.where(which == lower, 1.0, 0.0).astype(BF16)
        acc[...] += dot(lhs[...], hot[...], 1, 1)
        return c

    lax.fori_loop(0, NO, stack, 0)

    obuf[0, :, 0:128] = jnp.zeros((ROWS, 128), F32)
    fbuf[0, :, 0:128] = jnp.zeros((1, 128), F32)
    for zz in range(NZ):
        total = acc[zz * ROWS : (zz + 1) * ROWS] + acc[(NZ + zz) * ROWS : (NZ + zz + 1) * ROWS]
        folds = acc[2 * NZ * ROWS + zz : 2 * NZ * ROWS + zz + 1]
        obuf[zz, :, 128:] = total
        fbuf[zz, :, 128:] = folds
        if zz + 1 < NZ:
            obuf[zz + 1, :, 0:128] = total[:, GB - 128 :]
            fbuf[zz + 1, :, 0:128] = folds[:, GB - 128 :]

    def send_z(dz, c):
        zz = lax.rem(z + dz, NZ)
        remote(obuf.at[zz], obox.at[dz], bsend, brecv, at(zz, y, o)).start()
        remote(fbuf.at[zz], fbox.at[dz], fsend, frecv, at(zz, y, o)).start()
        return c

    lax.fori_loop(1, NZ, send_z, 0)
    total, folds = obuf[z], fbuf[z]
    await_bytes(fbox.at[pl.ds(1, NZ - 1)], frecv)
    for dz in range(1, NZ):
        folds = folds + fbox[dz]
    scale = 1.0 / jnp.sqrt(1.0 + folds)
    await_bytes(obox.at[pl.ds(1, NZ - 1)], brecv)
    for dz in range(1, NZ):
        total = total + obox[dz]
    normal = total * scale
    re, im = normal[:8], normal[8:]
    err_re, err_im = re[:, 128:], im[:, 128:]
    for lag in range(1, LAGS + 1):
        lag_re = pltpu.roll(re, lag, 1)[:, 128:]
        lag_im = pltpu.roll(im, lag, 1)[:, 128:]
        ar = jnp.concatenate([cb[lag - 1, 0:8]] * (GB // 128), axis=1)
        ai = jnp.concatenate([cb[lag - 1, 8:16]] * (GB // 128), axis=1)
        err_re = err_re - (ar * lag_re - ai * lag_im)
        err_im = err_im - (ar * lag_im + ai * lag_re)
    for tile in range(GB // 128):
        ebuf[tile, 0:8] = err_re[:, tile * 128 : (tile + 1) * 128]
        ebuf[tile, 8:16] = err_im[:, tile * 128 : (tile + 1) * 128]

    per_tile = 128 // BIN_DEV
    pltpu.make_async_copy(ebuf.at[lax.div(y, per_tile)], ebox.at[y], erecv).start()

    def send_y(dy, c):
        yy = lax.rem(y + dy, NY)
        remote(ebuf.at[lax.div(yy, per_tile)], ebox.at[y], esend, erecv, at(z, yy, o)).start()
        return c

    lax.fori_loop(1, NY, send_y, 0)
    await_bytes(ebox, erecv)
    rest = ebox[...].reshape(NY * ROWS, 128).T
    done = jnp.zeros((128, NY * ROWS), F32)
    for _ in range(3):
        high = rest.astype(BF16)
        rest = rest - high.astype(F32)
        done = done + dot(high, place[...], 1, 0)
    res[...] = done
    out[...] = res[pl.ds(pl.multiple_of(lax.rem(y, per_tile) * BIN_DEV, BIN_DEV), BIN_DEV), :]

    await_bytes(lab1.at[pl.ds(0, NO - 1)], l1s)
    await_bytes(lab2.at[pl.ds(0, NY - 1)], l2s)
    await_bytes(sbuf.at[pl.ds(0, NO * NY - 1)], asend)
    await_bytes(obuf.at[pl.ds(0, NZ - 1)], bsend)
    await_bytes(fbuf.at[pl.ds(0, NZ - 1)], fsend)
    await_bytes(ebox.at[pl.ds(0, NY - 1)], esend)


def on_device(traces, trace_dest, trace_bin, trace_class, trace_fold, filters, predictor):
    main, short, place = tables()
    vmem, far = pl.BlockSpec(memory_space=pltpu.VMEM), pl.BlockSpec(memory_space=pl.ANY)
    dma, box = pltpu.SemaphoreType.DMA, pltpu.VMEM
    return pl.pallas_call(
        kernel,
        out_shape=jax.ShapeDtypeStruct((BIN_DEV, NY * ROWS), F32),
        in_specs=[far] + [vmem] * 6 + [far, far, vmem],
        out_specs=vmem,
        scratch_shapes=[
            box((TR, SAMPLES), F32),
            box(main.shape, BF16),
            box(short.shape, BF16),
            box((2, 2 * TR, HALF), BF16),
            box((2 * TAPS, TR), F32),
            box((64, 2 * TR), F32),
            box((256, 2 * TR), BF16),
            box((2, TR), jnp.int32),
            box((NO, 2, TR), jnp.int32),
            box((NY, NO, 2, TR), jnp.int32),
            box((NO * NY, ROWS, TR), F32),
            box((NO * NY, ROWS, TR), F32),
            box((2 * NZ * ROWS + 16, NY * TR), BF16),
            box((GB, NY * TR), BF16),
            box((2 * NZ * ROWS + 16, GB), F32),
            box((NZ, ROWS, WIDE), F32),
            box((NZ, ROWS, WIDE), F32),
            box((NZ, 1, WIDE), F32),
            box((NZ, 1, WIDE), F32),
            box((GB // 128, ROWS, 128), F32),
            box((NY, ROWS, 128), F32),
            box((NY * ROWS, LAGS), F32),
            box((LAGS, ROWS, 128), F32),
            box((128, NY * ROWS), F32),
            dma,
            dma((NO,)),
            dma((NO,)),
            dma, dma, dma, dma, dma,
            dma((NO,)),
            dma, dma, dma, dma, dma, dma,
        ],
        compiler_params=pltpu.CompilerParams(
            collective_id=0, has_side_effects=True, vmem_limit_bytes=40 * 2**20
        ),
        cost_estimate=pl.CostEstimate(flops=2 * 10**9, bytes_accessed=5 * 10**6, transcendentals=0),
    )(
        traces, trace_dest.reshape(1, TR), trace_bin, trace_class, trace_fold, filters, predictor,
        jnp.asarray(main), jnp.asarray(short), jnp.asarray(place),
    )


def solution(mesh):
    in_specs = (
        P("off", "bin", None),
        P("off", "bin", None),
        P("off", "bin"),
        P("off", "bin"),
        P("off", "bin"),
        P(),
        P(None, "off"),
    )
    return jax.shard_map(
        on_device, mesh=mesh, in_specs=in_specs, out_specs=P("bin", "off"), check_vma=False
    )
```
